256 devices in a mesh: rep: 8 (over z_hi, y), tp: 32 (over x, z_lo, core).
Axes of the slice: x: 4, y: 4, z: 8 (z_hi: 2, z_lo: 4; z = z_hi * 4 + z_lo), core: 2. Of those that a mesh axis runs over, the one named last changes fastest.
Arguments:
- prompts: bfloat16 [32, 96, 8192], P('rep', None, 'tp'), may hold values from -6 to 6
- output_matrix: bfloat16 [8192, 8192], P('tp'), may hold values from -0.125 to 0.125
- adapter_weight_pair: bfloat16 [32, 8192, 128], P('tp'), may hold values from -0.1875 to 0.1875
- adapter: int32 [32], replicated, may hold values from 0 to 31
- lengths: int32 [32], replicated, may hold values from 1 to 96, 2304 in all
- placement: int32 [32, 1], replicated, may hold values from 0 to 7; in each aligned block of 4 rows (0 to 3, 4 to 7, ...) no two rows name the same one
Outputs:
- served: bfloat16 [8, 8, 96, 8192], P('rep', None, None, 'tp')
The draws below stay inside these ranges and needn't reach their ends.
Inputs may be any that keep to these rules, and one draw needn't show every extreme that they name: `placement`: among the 4 prompts of one index of rep, no group is named more than 1 times, a bound that some block reaches. `lengths`: the largest length equals 96.
All inputs are finite; a program needn't handle non-finite values.
Results may differ from the reference program's by a relative error of at most 0.0034.
Values may be sent and summed in bfloat16 or wider, within the bound.
A program may use at most 128 MiB of HBM per device.

```python
import math
import jax
import jax.numpy as jnp
import numpy as np

MODEL_WIDTH = 8192
ADAPTER_RANK = 64
PPG = 4
ROWS = 96
PROMPTS = 32
ADAPTER_TOTAL = 32
SEND_CAP = 1
SLOTS = 8
N_REP = 8


def set_ends(values, own_key, smallest, top_value):
    spot = [jax.random.randint(jax.random.fold_in(own_key, axis), (), 0, length) for axis, length in enumerate(values.shape)]
    main_axis = values.shape.index(max(values.shape))
    neighbour = spot[:main_axis] + [(spot[main_axis] + 1) % values.shape[main_axis]] + spot[main_axis + 1:]
    return values.at[tuple(spot)].set(smallest).at[tuple(neighbour)].set(top_value)


def raised(values, rng, source, target, parts, factor):
    def block_of(position):
        return (jnp.arange(values.shape[position]) // (values.shape[position] // parts)).reshape((-1,) + (1,) * (values.ndim - 1 - position))

    near = jax.random.permutation(rng, parts)[block_of(target)]
    far = (block_of(target) + parts // 2) % parts
    return jnp.where((block_of(source) == near) | (block_of(source) == far), factor * values, values)


def levels(rng, extent, split, smallest, largest):
    level = 1.0
    for dim, blocks in split:
        heights = jax.random.uniform(jax.random.fold_in(jax.random.fold_in(rng, 6), dim), (blocks,), jnp.float32, smallest / len(split), largest / len(split))
        level = level * jnp.repeat(jnp.exp(heights), extent[dim] // blocks).reshape((-1,) + (1,) * (len(extent) - 1 - dim))
    return level


def split_up(amount, total, most, skew):
    loads = [(1 << 20) // math.isqrt(standing ** skew) + 1 for standing in range(2, amount + 1)]
    spare, given = total - most - (amount - 1), [1] * (amount - 1)
    while spare > 0:
        movable = [i for i in range(amount - 1) if given[i] < most]
        whole, remaining = sum([loads[i] for i in movable]), spare
        for i in movable:
            more = min(most - given[i], max(1, remaining * loads[i] // whole), spare)
            given[i] = given[i] + more
            spare = spare - more
    return np.array([most] + given)


def ragged(own_key, amount, total, bound, skew):
    if amount == 2:
        one = jax.random.randint(own_key, (), max(1, total - bound), min(bound, total - 1) + 1)
        return jnp.stack([one, total - one])
    sizes = jnp.asarray(split_up(amount, total, bound, skew), jnp.int32)
    couples = (amount - 1) // 2
    source_of, receiver = sizes[1:1 + 2 * couples:2], sizes[2:2 + 2 * couples:2]
    margin = jnp.minimum(source_of - 1, bound - receiver)
    moved = jax.random.randint(jax.random.fold_in(own_key, 1), (couples,), 0, 1 << 20) % (margin + 1)
    sizes = sizes.at[1:1 + 2 * couples:2].set(source_of - moved).at[2:2 + 2 * couples:2].set(receiver + moved)
    return sizes[jax.random.permutation(jax.random.fold_in(own_key, 2), amount)]


def shared_out(key, own, number, rows, amount, top, bound, slope):
    ranking = jax.random.permutation(key, amount)
    packed, usual = load_shares(amount, rows * top, bound, slope, True), load_shares(amount, rows * top, bound, slope, False)
    places = jnp.arange(amount)

    def named(sizes, offset_by):
        used = int((sizes > 0).sum())
        fixed = max(1, used // 4)
        passed = fixed + (places - fixed + offset_by * (used - fixed)) % max(1, amount - fixed)
        return jnp.zeros((amount,), jnp.int32).at[ranking[jnp.where(places < fixed, places, passed)]].set(jnp.asarray(sizes, jnp.int32))

    sizes = jnp.where(number % 4 == 0, named(packed, number // 4), named(usual, number - number // 4 - 1))
    mixed = jax.random.permutation(jax.random.fold_in(own, 3), amount)
    donor, receiver = mixed[0:amount // 2 * 2:2], mixed[1:amount // 2 * 2:2]
    room = jnp.minimum(sizes[donor] - 1, bound - sizes[receiver]) // 2
    room = jnp.where((donor == ranking[0]) | (receiver == ranking[0]) | (sizes[receiver] == 0), 0, jnp.maximum(room, 0))
    passed = jax.random.randint(jax.random.fold_in(own, 4), (amount // 2,), 0, 1 << 20) % (room + 1)
    sizes = sizes.at[donor].add(-passed).at[receiver].add(passed)
    labels = jnp.searchsorted(jnp.cumsum(sizes), jnp.arange(rows * top), side="right").astype(jnp.int32)
    table = labels.reshape(top, rows).T
    table = table[jax.random.permutation(jax.random.fold_in(own, 1), rows)]
    offset_by = jax.random.randint(jax.random.fold_in(own, 2), (rows, 1), 0, top)
    return jnp.take_along_axis(table, (jnp.arange(top)[None, :] + offset_by) % top, axis=1)


def load_shares(count, total, bound, slope, full):
    portions = [(1 << 20) // math.isqrt(rank ** slope) + 1 for rank in range(1, count + 1)]
    largest = bound if full else min(bound, max(-(-total // count), total * portions[0] // sum(portions)))
    least = 1 if total - largest >= count - 1 else 0
    given, spare = [largest] + [least] * (count - 1), total - largest - least * (count - 1)
    while spare > 0:
        movable = [i for i in range(1, count) if given[i] < largest] or [i for i in range(1, count) if given[i] < bound]
        mass, budget = sum([portions[i] for i in movable]), spare
        for i in movable:
            extra = min(bound - given[i], max(1, budget * portions[i] // mass), spare)
            given[i] = given[i] + extra
            spare = spare - extra
    return np.array(given)


def bell_draw(rng, dims, spread, bound, pieces=(), held_as=jnp.bfloat16):
    drawn = spread * jax.random.normal(rng, dims, jnp.float32)
    if pieces:
        drawn = drawn * levels(rng, dims, pieces, -0.22, 0.18)
    return jnp.clip(drawn, -bound, bound).astype(held_as)


def noise_with(stream_key, dims, scale, most, shards, heavy, kind=jnp.bfloat16):
    values = scale * jax.random.normal(stream_key, dims, jnp.float32)
    if shards:
        values = values * levels(stream_key, dims, shards, -0.22, 0.18)
    return jnp.clip(raised(values, jax.random.fold_in(stream_key, 3), *heavy), -most, most).astype(kind)


def setup_inputs(seed: int = 0) -> dict:
    key_of = jax.random.split(jax.random.key(seed), 7)
    prompts = bell_draw(key_of[0], (PROMPTS, ROWS, MODEL_WIDTH), 1.0, 6.0, ((0, 8), (2, 32)))
    output_matrix = noise_with(key_of[1], (MODEL_WIDTH, MODEL_WIDTH), MODEL_WIDTH ** -0.5, 0.125, ((0, 32),), (0, 1, 32, 2.75))
    adapter_weight_pair = bell_draw(key_of[2], (ADAPTER_TOTAL, MODEL_WIDTH, 2 * ADAPTER_RANK), (MODEL_WIDTH // 8) ** -0.5, 0.1875, ((0, 32),))
    adapter = set_ends(jax.random.randint(key_of[3], (PROMPTS,), 0, ADAPTER_TOTAL), jax.random.fold_in(key_of[3], 1), 0, ADAPTER_TOTAL - 1).astype(jnp.int32)
    lengths = ragged(key_of[4], PROMPTS, PROMPTS * ROWS * 3 // 4, ROWS, 0).astype(jnp.int32)
    placement_keys = jax.random.split(jax.random.fold_in(key_of[5], 1), PROMPTS // PPG)
    placement_turns = jax.random.permutation(jax.random.fold_in(key_of[5], 3), PROMPTS // PPG)
    placement = jax.vmap(lambda own, number: shared_out(jax.random.fold_in(key_of[5], 2), own, number, PPG, N_REP, 1, SEND_CAP, 2))(placement_keys, placement_turns).reshape((PROMPTS, 1))
    return {"prompts": prompts, "output_matrix": output_matrix, "adapter_weight_pair": adapter_weight_pair, "adapter": adapter, "lengths": lengths, "placement": placement}


def reference(prompts, output_matrix, adapter_weight_pair, adapter, lengths, placement):
    flat = prompts.reshape(PROMPTS * ROWS, MODEL_WIDTH)
    base_sum = jnp.dot(flat, output_matrix, preferred_element_type=jnp.float32)
    picked_adapter = adapter_weight_pair[adapter]
    down = jnp.einsum("prf,pfk->prk", prompts.astype(jnp.float32), picked_adapter[:, :, :ADAPTER_RANK].astype(jnp.float32))
    down_b = down.astype(jnp.bfloat16)
    lifted = jnp.einsum("prk,pfk->prf", down_b.astype(jnp.float32), picked_adapter[:, :, ADAPTER_RANK:].astype(jnp.float32))
    live_rows = (jnp.arange(ROWS, dtype=jnp.int32)[None, :] < lengths[:, None]).astype(jnp.float32)
    result = ((base_sum.reshape(PROMPTS, ROWS, MODEL_WIDTH) + 0.5 * lifted) * live_rows[:, :, None]).astype(jnp.bfloat16)
    prompt_ids = jnp.arange(PROMPTS, dtype=jnp.int32)
    home_group = prompt_ids // PPG
    target = placement[:, 0]
    earlier = (home_group[:, None] == home_group[None, :]) & (target[:, None] == target[None, :]) & (prompt_ids[None, :] < prompt_ids[:, None])
    order_rank = jnp.sum(earlier.astype(jnp.int32), axis=1)
    slot_index = home_group * SEND_CAP + order_rank
    served = jnp.zeros((N_REP, SLOTS, ROWS, MODEL_WIDTH), jnp.bfloat16)
    return served.at[target, slot_index].set(result)
```

```python
import functools

import jax
import jax.numpy as jnp
from jax import lax
from jax.experimental import pallas as pl
from jax.experimental.pallas import tpu as pltpu
from jax.sharding import PartitionSpec as P

MESH = pl.DeviceIdType.MESH
BF = jnp.bfloat16
F32 = jnp.float32

NX, NZ, NC = 4, 4, 2
NY, NH = 4, 2


def kernel(
    adapter_s, lengths_s, target_s, x_ref, w_ref, a_ref, out_ref,
    x_sib, w_own, w_sib,
    s_far, s_dir, s_acc, r_far, r_dir, r_acc,
    s_z, r_z, base,
    lib, s_sel, sel, dpack, r_sib, x_sum, z_sum, down, r_down,
    s_out,
    w_own_sem, w_send, w_recv, x_send, x_recv,
    far_send, far_recv, dir_send, dir_recv, acc_send, acc_recv,
    z_send, z_recv,
    lib_own, lib_send, lib_recv, sel_send, sel_recv,
    down_send, down_recv, out_send, out_recv,
):
    rep = lax.axis_index("rep")
    tp = lax.axis_index("tp")
    hi, y = rep // NY, rep % NY
    x = tp // (NZ * NC)
    zl = (tp // NC) % NZ
    core = tp % NC
    tps, reps = NX * NZ * NC, NY * NH
    prompts, rows = out_ref.shape[0] // 2, out_ref.shape[1]
    width = out_ref.shape[2]
    share = width // NY

    def tp_of(xx, zz, cc):
        return (xx * NZ + zz) * NC + cc

    def copy(src, dst, send, recv, r=None, t=None):
        return pltpu.make_async_remote_copy(
            src_ref=src, dst_ref=dst, send_sem=send, recv_sem=recv,
            device_id=(rep if r is None else r, tp if t is None else t),
            device_id_type=MESH,
        )

    sib = tp_of(x, zl, 1 - core)

    barrier = pltpu.get_barrier_semaphore()

    @pl.loop(1, tps)
    def _(j):
        pl.semaphore_signal(barrier, inc=1, device_id=(rep, (tp + j) % tps), device_id_type=MESH)

    @pl.loop(1, reps)
    def _(j):
        pl.semaphore_signal(barrier, inc=1, device_id=((rep + j) % reps, tp), device_id_type=MESH)

    def w_columns(d, q, cc):
        start = tp_of((x + d) % NX, q, cc) * width
        return w_ref.at[:, pl.ds(pl.multiple_of(start, width), width)]

    order = (2, 1, 3, 0)
    pairs = (0, 3, 1, 2)
    own_copies = {}
    for d in order:
        for q in pairs:
            own_copies[d, q] = pltpu.make_async_copy(
                w_columns(d, q, core), w_own.at[d, q], w_own_sem.at[d, q]
            )
            own_copies[d, q].start()
    lib_copy = pltpu.make_async_copy(
        a_ref.at[pl.ds(pl.multiple_of(tp * width + y * share, share), share), :], lib.at[tp], lib_own
    )
    lib_copy.start()

    pl.semaphore_wait(barrier, tps - 1 + reps - 1)

    x_copy = copy(x_ref, x_sib, x_send, x_recv, t=sib)
    x_copy.start()
    w_copies = {}
    for d in order:
        for q in pairs:
            w_copies[d, q] = copy(
                w_columns(d, q, 1 - core), w_sib.at[d, q], w_send.at[d, q], w_recv.at[d, q], t=sib
            )
            w_copies[d, q].start()

    @pl.loop(1, tps)
    def _(j):
        to = (tp + j) % tps
        copy(
            a_ref.at[pl.ds(pl.multiple_of(to * width + y * share, share), share), :],
            lib.at[tp], lib_send, lib_recv, t=to,
        ).start()

    ready = set()

    def partial(d, q):
        if not ready:
            x_copy.wait_recv()
        if (d, q) not in ready:
            own_copies[d, q].wait()
            w_copies[d, q].wait_recv()
            ready.add((d, q))
        return jnp.dot(x_ref[...], w_own[d, q], preferred_element_type=F32) + jnp.dot(
            x_sib[...], w_sib[d, q], preferred_element_type=F32
        )

    def way(q):
        return 1 if q < NZ // 2 else 3

    fars, dirs, accs, zs = {}, {}, {}, {}

    def far_step(q):
        s_far[q] = partial(2, q).astype(BF)
        fars[q] = copy(
            s_far.at[q], r_far.at[q], far_send.at[q], far_recv.at[q],
            t=tp_of((x + way(q)) % NX, zl, core),
        )
        fars[q].start()

    def dir_step(q):
        d = NX - way(q)
        s_dir[q] = partial(d, q).astype(BF)
        dirs[q] = copy(
            s_dir.at[q], r_dir.at[q], dir_send.at[q], dir_recv.at[q],
            t=tp_of((x + d) % NX, zl, core),
        )
        dirs[q].start()

    def acc_step(q):
        d = way(q)
        own = partial(d, q)
        fars[q].wait_recv()
        s_acc[q] = (own + r_far[q].astype(F32)).astype(BF)
        accs[q] = copy(
            s_acc.at[q], r_acc.at[q], acc_send.at[q], acc_recv.at[q],
            t=tp_of((x + d) % NX, zl, core),
        )
        accs[q].start()

    def z_step(q):
        own = partial(0, q)
        dirs[q].wait_recv()
        accs[q].wait_recv()
        total = own + r_dir[q].astype(F32) + r_acc[q].astype(F32)

        @pl.when(q == zl)
        def _():
            base[...] = total

        zs[q] = copy(
            s_z.at[q], r_z.at[zl], z_send.at[q], z_recv.at[zl], t=tp_of(x, q, core)
        )

        @pl.when(q != zl)
        def _():
            s_z[q] = total.astype(BF)
            zs[q].start()

    for q in (0, 3):
        far_step(q)
    for q in (0, 3):
        dir_step(q)
    for q in (0, 3):
        acc_step(q)
    for q in (1, 2):
        far_step(q)
    for q in (1, 2):
        dir_step(q)

    lib_copy.wait()
    lib_all = copy(
        lib.at[pl.ds(0, tps - 1)], lib.at[pl.ds(0, tps - 1)], lib_send, lib_recv, t=sib
    )
    lib_all.wait_recv()
    sels = []
    for j in range(1, NY):
        to = hi * NY + (y + j) % NY
        for p in range(prompts):
            s_sel[j, p] = lib[adapter_s[to * prompts + p]]
        sels.append(copy(
            s_sel.at[j], sel.at[:, y], sel_send.at[j], sel_recv.at[y], r=to
        ))
        sels[-1].start()
    for p in range(prompts):
        sel[p, y] = lib[adapter_s[rep * prompts + p]]

    for q in (0, 3):
        z_step(q)

    for j in range(1, NY):
        fr = (y + j) % NY
        copy(s_sel.at[j], sel.at[:, fr], sel_send.at[j], sel_recv.at[fr], r=hi * NY + fr).wait_recv()

    def chosen(p):
        return sel[p].reshape(width, sel.shape[3])

    rank = sel.shape[3] // 2
    for k in range(2):
        parts = [
            jnp.dot(
                x_ref[pl.ds((2 * k + i) * rows, rows), :], chosen(2 * k + i),
                preferred_element_type=F32,
            )
            for i in range(2)
        ]
        dpack[k] = jnp.concatenate([parts[0][:, :rank], parts[1][:, :rank]], axis=1)
    sib_copy = copy(dpack.at[1 - core], r_sib, down_send.at[0], down_recv.at[0], t=sib)
    sib_copy.start()

    for q in (1, 2):
        acc_step(q)

    sib_copy.wait_recv()
    x_sum[x] = dpack[core] + r_sib[...]
    d_copies = []
    for j in range(1, NX):
        c = copy(
            x_sum.at[x], x_sum.at[x], down_send.at[j], down_recv.at[1 + x],
            t=tp_of((x + j) % NX, zl, core),
        )
        c.start()
        d_copies.append(c)
    for j in range(1, NX):
        fr = (x + j) % NX
        copy(
            x_sum.at[fr], x_sum.at[fr], down_send.at[j], down_recv.at[1 + fr],
            t=tp_of(fr, zl, core),
        ).wait_recv()
    z_sum[zl] = (x_sum[0] + x_sum[1]) + (x_sum[2] + x_sum[3])
    for j in range(1, NZ):
        c = copy(
            z_sum.at[zl], z_sum.at[zl], down_send.at[NX - 1 + j], down_recv.at[1 + NX + zl],
            t=tp_of(x, (zl + j) % NZ, core),
        )
        c.start()
        d_copies.append(c)

    for q in (1, 2):
        z_step(q)

    for j in range(1, NZ):
        fr = (zl + j) % NZ
        copy(
            z_sum.at[fr], z_sum.at[fr], down_send.at[NX - 1 + j], down_recv.at[1 + NX + fr],
            t=tp_of(x, fr, core),
        ).wait_recv()
    down[...] = ((z_sum[0] + z_sum[1]) + (z_sum[2] + z_sum[3])).astype(BF)
    back = copy(down, r_down, down_send.at[NX + NZ - 1], down_recv.at[1 + NX + NZ], t=sib)
    back.start()
    back.wait_recv()

    mine, other = down[...], r_down[...]
    packs = [jnp.where(core == 0, mine, other), jnp.where(core == 0, other, mine)]
    lanes = lax.broadcasted_iota(jnp.int32, (rows, 2 * rank), 1)
    row_ids = lax.broadcasted_iota(jnp.int32, (rows, width), 0)
    lifted = []
    for p in range(prompts):
        pack = packs[p // 2].astype(F32)
        if p % 2 == 0:
            pack = jnp.concatenate([pack[:, rank:], pack[:, :rank]], axis=1)
        pack = jnp.where(lanes >= rank, pack, 0.0).astype(BF)
        lifted.append(0.5 * lax.dot_general(
            pack, chosen(p), (((1,), (1,)), ((), ())), preferred_element_type=F32
        ))

    for j in range(1, NZ):
        fr = (zl + j) % NZ
        copy(
            s_z.at[0], r_z.at[fr], z_send.at[0], z_recv.at[fr], t=tp_of(x, fr, core)
        ).wait_recv()
    results = []
    for p in range(prompts):
        span = pl.ds(p * rows, rows)
        total = base[span, :] + lifted[p]
        for j in range(1, NZ):
            total += r_z[(zl + j) % NZ, span, :].astype(F32)
        live = row_ids < lengths_s[rep * prompts + p]
        results.append(jnp.where(live, total, 0.0))

    outs = []
    for j in range(reps):
        to = (rep + j) % reps
        value = jnp.zeros((rows, width), F32)
        for p in range(prompts):
            value = jnp.where(target_s[rep * prompts + p] == to, results[p], value)
        if j == 0:
            out_ref[rep] = value.astype(BF)
        else:
            s_out[j] = value.astype(BF)
            outs.append(copy(
                s_out.at[j], out_ref.at[rep], out_send.at[j], out_recv.at[rep], r=to
            ))
            outs[-1].start()

    x_copy.wait_send()
    for c in w_copies.values():
        c.wait_send()
    lib_all.wait_send()
    for group in (fars, dirs, accs):
        for c in group.values():
            c.wait_send()
    for q in range(NZ):
        @pl.when(q != zl)
        def _(q=q):
            zs[q].wait_send()
    for c in sels + [sib_copy, back] + d_copies + outs:
        c.wait_send()
    for j in range(1, reps):
        fr = (rep + j) % reps
        copy(s_out.at[j], out_ref.at[fr], out_send.at[j], out_recv.at[fr], r=fr).wait_recv()


def local(prompts, output_matrix, adapter_weight_pair, adapter, lengths, placement):
    count, rows, width = prompts.shape
    reps = lax.axis_size("rep")
    tps = lax.axis_size("tp")
    pair = adapter_weight_pair.shape[2]
    tall = count * rows
    dma = pltpu.SemaphoreType.DMA
    smem = pl.BlockSpec(memory_space=pltpu.SMEM)
    vmem = pl.BlockSpec(memory_space=pltpu.VMEM)
    hbm = pl.BlockSpec(memory_space=pl.ANY)
    block = pltpu.VMEM((NZ, tall, width), BF)
    out = pl.pallas_call(
        kernel,
        out_shape=jax.ShapeDtypeStruct((reps, rows, width), BF),
        in_specs=[smem, smem, smem, vmem, hbm, hbm],
        out_specs=vmem,
        scratch_shapes=[
            pltpu.VMEM((tall, width), BF),
            pltpu.VMEM((NX, NZ, width, width), BF),
            pltpu.VMEM((NX, NZ, width, width), BF),
            block, block, block, block, block, block,
            block, block, pltpu.VMEM((tall, width), F32),
            pltpu.VMEM((tps, width // NY, pair), BF),
            pltpu.VMEM((NY, count, width // NY, pair), BF),
            pltpu.VMEM((count, NY, width // NY, pair), BF),
            pltpu.VMEM((2, rows, pair), F32),
            pltpu.VMEM((rows, pair), F32),
            pltpu.VMEM((NX, rows, pair), F32),
            pltpu.VMEM((NZ, rows, pair), F32),
            pltpu.VMEM((rows, pair), BF),
            pltpu.VMEM((rows, pair), BF),
            pltpu.VMEM((reps, rows, width), BF),
            dma((NX, NZ)), dma((NX, NZ)), dma((NX, NZ)), dma, dma,
            dma((NZ,)), dma((NZ,)), dma((NZ,)), dma((NZ,)), dma((NZ,)), dma((NZ,)),
            dma((NZ,)), dma((NZ,)),
            dma, dma, dma, dma((NY,)), dma((NY,)),
            dma((NX + NZ,)), dma((2 + NX + NZ,)), dma((reps,)), dma((reps,)),
        ],
        compiler_params=pltpu.CompilerParams(
            collective_id=0, has_side_effects=True, vmem_limit_bytes=48 * 1024 * 1024
        ),
    )(
        adapter, lengths, placement.reshape(-1), prompts.reshape(tall, width), output_matrix,
        adapter_weight_pair.reshape(-1, pair),
    )
    return out[None]


def solution(mesh):
    in_specs = (P("rep", None, "tp"), P("tp", None), P("tp", None, None), P(), P(), P())
    out_specs = P("rep", None, None, "tp")
    return jax.shard_map(local, mesh=mesh, in_specs=in_specs, out_specs=out_specs, check_vma=False)
```

```python
import functools

import jax
import jax.numpy as jnp
from jax import lax
from jax.experimental import pallas as pl
from jax.experimental.pallas import tpu as pltpu
from jax.sharding import PartitionSpec as P

MESH = pl.DeviceIdType.MESH
BF = jnp.bfloat16
F32 = jnp.float32

NX, NZ, NC = 4, 4, 2
NY, NH = 4, 2
FAR_FIRST = (6, 2, 5, 7, 4, 1, 3, 0)
SCHEDULE = (
    "W0", "lib", "F0", "W1", "W2", "W3", "D0", "C0", "F1", "D1", "S0", "C1", "choose", "F2",
    "D2", "S1", "C2", "down", "F3", "D3", "S2", "down_z", "C3", "S3", "down_back", "lift", "O0", "O1",
)


def kernel(
    adapter_h, lengths_h, target_h, x_hbm, w_ref, a_ref, out_ref,
    adapter_s, lengths_s, target_s, x_ref, x_sib, w_own, w_sib,
    s_far, s_dir, s_acc, r_far, r_dir, r_acc,
    s_z, r_z, base,
    lib, s_sel, sel, dpack, x_sum, z_sum, down, lifted,
    s_out,
    in_sem, w_own_sem, w_send, w_recv, x_send, x_recv,
    far_send, far_recv, dir_send, dir_recv, acc_send, acc_recv,
    z_send, z_recv,
    lib_own, lib_send, lib_recv, sel_send, sel_recv,
    down_send, down_recv, out_send, out_recv,
):
    rep = lax.axis_index("rep")
    tp = lax.axis_index("tp")
    hi, y = rep // NY, rep % NY
    x = tp // (NZ * NC)
    zl = (tp // NC) % NZ
    core = tp % NC
    tps, reps = NX * NZ * NC, NY * NH
    prompts, rows = out_ref.shape[0] // 2, out_ref.shape[1]
    width = out_ref.shape[2]
    share, half = width // NY, width // 2

    def tp_of(xx, zz, cc):
        return (xx * NZ + zz) * NC + cc

    def copy(src, dst, send, recv, r=None, t=None):
        return pltpu.make_async_remote_copy(
            src_ref=src, dst_ref=dst, send_sem=send, recv_sem=recv,
            device_id=(rep if r is None else r, tp if t is None else t),
            device_id_type=MESH,
        )

    sib = tp_of(x, zl, 1 - core)

    barrier = pltpu.get_barrier_semaphore()

    @pl.loop(1, tps)
    def _(j):
        pl.semaphore_signal(barrier, inc=1, device_id=(rep, (tp + j) % tps), device_id_type=MESH)

    @pl.loop(1, reps)
    def _(j):
        pl.semaphore_signal(barrier, inc=1, device_id=((rep + j) % reps, tp), device_id_type=MESH)

    def w_columns(d, q, cc):
        start = tp_of((x + d) % NX, q, cc) * width
        return w_ref.at[:, pl.ds(pl.multiple_of(start, width), width)]

    def way(q):
        return 1 if q < NZ // 2 else 3

    pairs = ((0, 3), (1, 2))
    order = []
    for pair in pairs:
        order += [(2, q) for q in pair] + [(NX - way(q), q) for q in pair]
    for pair in pairs:
        order += [(way(q), q) for q in pair]
    order += [(0, q) for pair in pairs for q in pair]
    x_load = pltpu.make_async_copy(x_hbm, x_ref, in_sem.at[0])
    x_load.start()
    tables = [
        pltpu.make_async_copy(src, dst, in_sem.at[i + 1])
        for i, (src, dst) in enumerate(
            ((adapter_h, adapter_s), (lengths_h, lengths_s), (target_h, target_s))
        )
    ]
    for c in tables:
        c.start()
    own_copies = {}
    for d, q in order:
        own_copies[d, q] = pltpu.make_async_copy(
            w_columns(d, q, core), w_own.at[d, q], w_own_sem.at[d, q]
        )
        own_copies[d, q].start()
    lib_copy = pltpu.make_async_copy(
        a_ref.at[pl.ds(pl.multiple_of(tp * width + y * share, share), share), :], lib.at[tp], lib_own
    )

    pl.semaphore_wait(barrier, tps - 1 + reps - 1)

    x_copy = copy(x_hbm, x_sib, x_send, x_recv, t=sib)
    x_copy.start()
    w_copies = {}
    for d, q in order:
        w_copies[d, q] = copy(
            w_columns(d, q, 1 - core), w_sib.at[d, q], w_send.at[d, q], w_recv.at[d, q], t=sib
        )

    def w_step(i):
        for key in order[4 * i:4 * i + 4]:
            w_copies[key].start()

    ready = set()

    def inputs(d, q):
        if not ready:
            x_load.wait()
            x_copy.wait_recv()
        if (d, q) not in ready:
            own_copies[d, q].wait()
            w_copies[d, q].wait_recv()
            ready.add((d, q))

    def partial(d, q, h=None):
        inputs(d, q)
        cols = slice(None) if h is None else pl.ds(h * half, half)
        return jnp.dot(x_ref[...], w_own[d, q, :, cols], preferred_element_type=F32) + jnp.dot(
            x_sib[...], w_sib[d, q, :, cols], preferred_element_type=F32
        )

    fars, dirs, accs, zs = {}, {}, {}, {}
    filled = set()

    def both_halves(buf, d, q):
        if (d, q) in filled:
            return
        filled.add((d, q))
        whole = partial(d, q).astype(BF)
        for h in range(2):
            buf[q, h] = whole[:, h * half:(h + 1) * half]

    def far_step(q, h):
        both_halves(s_far, 2, q)
        fars[q, h] = copy(
            s_far.at[q, h], r_far.at[q, h], far_send.at[q, h], far_recv.at[q, h],
            t=tp_of((x + way(q)) % NX, zl, core),
        )
        fars[q, h].start()

    def dir_step(q, h):
        d = NX - way(q)
        both_halves(s_dir, d, q)
        dirs[q, h] = copy(
            s_dir.at[q, h], r_dir.at[q, h], dir_send.at[q, h], dir_recv.at[q, h],
            t=tp_of((x + d) % NX, zl, core),
        )
        dirs[q, h].start()

    def acc_step(q, h):
        d = way(q)
        own = partial(d, q, h)
        fars[q, h].wait_recv()
        s_acc[q, h] = (own + r_far[q, h].astype(F32)).astype(BF)
        accs[q, h] = copy(
            s_acc.at[q, h], r_acc.at[q, h], acc_send.at[q, h], acc_recv.at[q, h],
            t=tp_of((x + d) % NX, zl, core),
        )
        accs[q, h].start()

    def z_step(q, h):
        own = partial(0, q, h)
        dirs[q, h].wait_recv()
        accs[q, h].wait_recv()
        total = own + r_dir[q, h].astype(F32) + r_acc[q, h].astype(F32)

        @pl.when(q == zl)
        def _():
            base[h] = total

        zs[q, h] = copy(
            s_z.at[q, h], r_z.at[zl, h], z_send.at[q, h], z_recv.at[zl, h], t=tp_of(x, q, core)
        )

        @pl.when(q != zl)
        def _():
            s_z[q, h] = total.astype(BF)
            zs[q, h].start()

    lib_all = copy(
        lib.at[pl.ds(0, tps - 1)], lib.at[pl.ds(0, tps - 1)], lib_send, lib_recv, t=sib
    )
    waits = []

    def lib_step():
        lib_copy.start()
        waits.append(lib_all)

        @pl.loop(1, tps)
        def _(j):
            to = (tp + j) % tps
            copy(
                a_ref.at[pl.ds(pl.multiple_of(to * width + y * share, share), share), :],
                lib.at[tp], lib_send, lib_recv, t=to,
            ).start()

    def choose_step():
        lib_copy.wait()
        lib_all.wait_recv()
        for j in range(1, NY):
            to = hi * NY + (y + j) % NY
            for p in range(prompts):
                s_sel[j, p] = lib[adapter_s[to * prompts + p]]
            c = copy(s_sel.at[j], sel.at[:, y], sel_send.at[j], sel_recv.at[y], r=to)
            c.start()
            waits.append(c)
        for p in range(prompts):
            sel[p, y] = lib[adapter_s[rep * prompts + p]]

    def chosen(p):
        return sel[p].reshape(width, sel.shape[3])

    rank = sel.shape[3] // 2
    thin = rows // NX
    line, place = NX * NC, x * NC + core

    def peer(j):
        other = (place + j) % line
        return other, tp_of(other // NC, zl, other % NC)

    def thin_rows(xx):
        return pl.ds(pl.multiple_of(xx * thin, thin), thin)

    def down_step():
        for j in range(1, NY):
            fr = (y + j) % NY
            copy(
                s_sel.at[j], sel.at[:, fr], sel_send.at[j], sel_recv.at[fr], r=hi * NY + fr
            ).wait_recv()
        for k in range(2):
            parts = [
                jnp.dot(
                    x_ref[pl.ds((2 * k + i) * rows, rows), :], chosen(2 * k + i),
                    preferred_element_type=F32,
                )
                for i in range(2)
            ]
            dpack[k] = jnp.concatenate([parts[0][:, :rank], parts[1][:, :rank]], axis=1)
        for j in range(1, line):
            other, to = peer(j)
            c = copy(
                dpack.at[other % NC, thin_rows(other // NC)], x_sum.at[place],
                down_send.at[j], down_recv.at[place], t=to,
            )
            c.start()
            waits.append(c)

    def down_z_step():
        total = dpack[core, thin_rows(x)]
        for j in range(1, line):
            other, to = peer(j)
            copy(
                dpack.at[core, thin_rows(x)], x_sum.at[other], down_send.at[j], down_recv.at[other], t=to
            ).wait_recv()
            total += x_sum[other]
        z_sum[zl] = total
        for j in range(1, NZ):
            c = copy(
                z_sum.at[zl], z_sum.at[zl], down_send.at[line + j], down_recv.at[line + zl],
                t=tp_of(x, (zl + j) % NZ, core),
            )
            c.start()
            waits.append(c)

    def down_back_step():
        for j in range(1, NZ):
            fr = (zl + j) % NZ
            copy(
                z_sum.at[fr], z_sum.at[fr], down_send.at[line + j], down_recv.at[line + fr],
                t=tp_of(x, fr, core),
            ).wait_recv()
        down[core, thin_rows(x)] = (z_sum[0] + z_sum[1]) + (z_sum[2] + z_sum[3])
        for j in range(1, line):
            other, to = peer(j)
            mine = down.at[core, thin_rows(x)]
            c = copy(
                mine, mine, down_send.at[line + NZ + j], down_recv.at[line + NZ + place], t=to
            )
            c.start()
            waits.append(c)

    def lift_step():
        for j in range(1, line):
            other, to = peer(j)
            theirs = down.at[other % NC, thin_rows(other // NC)]
            copy(
                theirs, theirs, down_send.at[line + NZ + j], down_recv.at[line + NZ + other], t=to
            ).wait_recv()
        lanes = lax.broadcasted_iota(jnp.int32, (rows, 2 * rank), 1)
        for p in range(prompts):
            pack = down[p // 2]
            if p % 2 == 0:
                pack = jnp.concatenate([pack[:, rank:], pack[:, :rank]], axis=1)
            pack = jnp.where(lanes >= rank, pack, 0.0).astype(BF)
            lift = 0.5 * lax.dot_general(
                pack, chosen(p), (((1,), (1,)), ((), ())), preferred_element_type=F32
            )
            for h in range(2):
                lifted[h, pl.ds(p * rows, rows), :] = lift[:, h * half:(h + 1) * half]

    outs = []

    def out_step(h):
        for j in range(1, NZ):
            fr = (zl + j) % NZ
            copy(
                s_z.at[0, h], r_z.at[fr, h], z_send.at[0, h], z_recv.at[fr, h], t=tp_of(x, fr, core)
            ).wait_recv()
        row_ids = lax.broadcasted_iota(jnp.int32, (rows, half), 0)
        results = []
        for p in range(prompts):
            span = pl.ds(p * rows, rows)
            total = base[h, span, :] + lifted[h, span, :]
            for j in range(1, NZ):
                total += r_z[(zl + j) % NZ, h, span, :].astype(F32)
            live = row_ids < lengths_s[rep * prompts + p]
            results.append(jnp.where(live, total, 0.0))
        cols = pl.ds(h * half, half)
        for j in FAR_FIRST:
            to = (rep + j) % reps
            value = jnp.zeros((rows, half), F32)
            for p in range(prompts):
                value = jnp.where(target_s[rep * prompts + p] == to, results[p], value)
            if j == 0:
                out_ref[rep, :, cols] = value.astype(BF)
            else:
                s_out[j, h] = value.astype(BF)
                c = copy(
                    s_out.at[j, h], out_ref.at[rep, :, cols], out_send.at[j, h], out_recv.at[rep, h], r=to
                )
                c.start()
                outs.append(c)

    for c in tables:
        c.wait()
    rounds = [(h, pair) for h in range(2) for pair in pairs]
    base_steps = {"F": far_step, "D": dir_step, "C": acc_step, "S": z_step}
    other_steps = {
        "lib": lib_step, "choose": choose_step, "down": down_step,
        "down_z": down_z_step, "down_back": down_back_step, "lift": lift_step,
    }
    for step in SCHEDULE:
        if step[0] == "W":
            w_step(int(step[1]))
        elif step[0] in base_steps:
            h, pair = rounds[int(step[1])]
            for q in pair:
                base_steps[step[0]](q, h)
        elif step[0] == "O":
            out_step(int(step[1]))
        else:
            other_steps[step]()

    x_copy.wait_send()
    for c in w_copies.values():
        c.wait_send()
    for group in (fars, dirs, accs):
        for c in group.values():
            c.wait_send()
    for q in range(NZ):
        @pl.when(q != zl)
        def _(q=q):
            for h in range(2):
                zs[q, h].wait_send()
    for c in waits + outs:
        c.wait_send()
    for h in range(2):
        for j in range(1, reps):
            fr = (rep + j) % reps
            copy(
                s_out.at[j, h], out_ref.at[fr, :, pl.ds(h * half, half)],
                out_send.at[j, h], out_recv.at[fr, h], r=fr,
            ).wait_recv()


def local(prompts, output_matrix, adapter_weight_pair, adapter, lengths, placement):
    count, rows, width = prompts.shape
    reps = lax.axis_size("rep")
    tps = lax.axis_size("tp")
    pair = adapter_weight_pair.shape[2]
    tall = count * rows
    dma = pltpu.SemaphoreType.DMA
    vmem = pl.BlockSpec(memory_space=pltpu.VMEM)
    hbm = pl.BlockSpec(memory_space=pltpu.HBM)
    table = pltpu.SMEM((adapter.shape[0],), jnp.int32)
    block = pltpu.VMEM((NZ, 2, tall, width // 2), BF)
    out = pl.pallas_call(
        kernel,
        out_shape=jax.ShapeDtypeStruct((reps, rows, width), BF),
        in_specs=[hbm] * 6,
        out_specs=vmem,
        scratch_shapes=[
            table, table, table,
            pltpu.VMEM((tall, width), BF),
            pltpu.VMEM((tall, width), BF),
            pltpu.VMEM((NX, NZ, width, width), BF),
            pltpu.VMEM((NX, NZ, width, width), BF),
            block, block, block, block, block, block,
            block, block, pltpu.VMEM((2, tall, width // 2), F32),
            pltpu.VMEM((tps, width // NY, pair), BF),
            pltpu.VMEM((NY, count, width // NY, pair), BF),
            pltpu.VMEM((count, NY, width // NY, pair), BF),
            pltpu.VMEM((2, rows, pair), F32),
            pltpu.VMEM((NX * NC, rows // NX, pair), F32),
            pltpu.VMEM((NZ, rows // NX, pair), F32),
            pltpu.VMEM((2, rows, pair), F32),
            pltpu.VMEM((2, tall, width // 2), F32),
            pltpu.VMEM((reps, 2, rows, width // 2), BF),
            dma((4,)), dma((NX, NZ)), dma((NX, NZ)), dma((NX, NZ)), dma, dma,
            dma((NZ, 2)), dma((NZ, 2)), dma((NZ, 2)), dma((NZ, 2)), dma((NZ, 2)), dma((NZ, 2)),
            dma((NZ, 2)), dma((NZ, 2)),
            dma, dma, dma, dma((NY,)), dma((NY,)),
            dma((2 * NX * NC + NZ,)), dma((2 * NX * NC + NZ,)), dma((reps, 2)), dma((reps, 2)),
        ],
        compiler_params=pltpu.CompilerParams(
            collective_id=0, has_side_effects=True, vmem_limit_bytes=60 * 1024 * 1024
        ),
    )(
        adapter, lengths, placement.reshape(-1), prompts.reshape(tall, width), output_matrix,
        adapter_weight_pair.reshape(-1, pair),
    )
    return out[None]


def solution(mesh):
    in_specs = (P("rep", None, "tp"), P("tp", None), P("tp", None, None), P(), P(), P())
    out_specs = P("rep", None, None, "tp")
    return jax.shard_map(local, mesh=mesh, in_specs=in_specs, out_specs=out_specs, check_vma=False)
```

```python
import functools

import jax
import jax.numpy as jnp
from jax import lax
from jax.experimental import pallas as pl
from jax.experimental.pallas import tpu as pltpu
from jax.sharding import PartitionSpec as P

MESH = pl.DeviceIdType.MESH
BF = jnp.bfloat16
F32 = jnp.float32

NX, NZ, NC = 4, 4, 2
NY, NH = 4, 2
FAR_FIRST = (6, 5, 7, 4, 2, 1, 3, 0)
SCHEDULE = (
    "W0", "lib", "F0", "W1", "W2", "W3", "D0", "C0", "F1", "D1", "S0", "C1", "choose", "F2",
    "D2", "C2", "S1", "down", "F3", "D3", "S2", "down_z", "C3", "S3", "down_back", "lift", "O0", "O1",
)


def kernel(
    adapter_h, lengths_h, target_h, x_hbm, w_ref, a_ref, out_ref,
    adapter_s, lengths_s, target_s, x_ref, x_sib, w_own, w_sib,
    s_far, s_dir, s_acc, r_far, r_dir, r_acc,
    s_z, r_z, base,
    lib, s_sel, sel, dpack, x_sum, z_sum, down, lifted,
    s_out,
    in_sem, w_own_sem, w_send, w_recv, x_send, x_recv,
    far_send, far_recv, dir_send, dir_recv, acc_send, acc_recv,
    z_send, z_recv,
    lib_own, lib_send, lib_recv, sel_send, sel_recv,
    down_send, down_recv, out_send, out_recv,
):
    rep = lax.axis_index("rep")
    tp = lax.axis_index("tp")
    hi, y = rep // NY, rep % NY
    x = tp // (NZ * NC)
    zl = (tp // NC) % NZ
    core = tp % NC
    tps, reps = NX * NZ * NC, NY * NH
    prompts, rows = out_ref.shape[0] // 2, out_ref.shape[1]
    width = out_ref.shape[2]
    share, half = width // NY, width // 2

    def tp_of(xx, zz, cc):
        return (xx * NZ + zz) * NC + cc

    def copy(src, dst, send, recv, r=None, t=None):
        return pltpu.make_async_remote_copy(
            src_ref=src, dst_ref=dst, send_sem=send, recv_sem=recv,
            device_id=(rep if r is None else r, tp if t is None else t),
            device_id_type=MESH,
        )

    sib = tp_of(x, zl, 1 - core)

    barrier = pltpu.get_barrier_semaphore()

    @pl.loop(1, tps)
    def _(j):
        pl.semaphore_signal(barrier, inc=1, device_id=(rep, (tp + j) % tps), device_id_type=MESH)

    @pl.loop(1, reps)
    def _(j):
        pl.semaphore_signal(barrier, inc=1, device_id=((rep + j) % reps, tp), device_id_type=MESH)

    def w_columns(d, q, cc):
        start = tp_of((x + d) % NX, q, cc) * width
        return w_ref.at[:, pl.ds(pl.multiple_of(start, width), width)]

    def way(q):
        return 1 if q < NZ // 2 else 3

    pairs = ((0, 3), (1, 2))
    order = []
    for pair in pairs:
        order += [(2, q) for q in pair] + [(NX - way(q), q) for q in pair]
    for pair in pairs:
        order += [(way(q), q) for q in pair]
    order += [(0, q) for pair in pairs for q in pair]
    x_load = pltpu.make_async_copy(x_hbm, x_ref, in_sem.at[0])
    x_load.start()
    tables = [
        pltpu.make_async_copy(src, dst, in_sem.at[i + 1])
        for i, (src, dst) in enumerate(
            ((adapter_h, adapter_s), (lengths_h, lengths_s), (target_h, target_s))
        )
    ]
    for c in tables:
        c.start()
    own_copies = {}
    for d, q in order:
        own_copies[d, q] = pltpu.make_async_copy(
            w_columns(d, q, core), w_own.at[d, q], w_own_sem.at[d, q]
        )
        own_copies[d, q].start()
    lib_copy = pltpu.make_async_copy(
        a_ref.at[pl.ds(pl.multiple_of(tp * width + y * share, share), share), :], lib.at[tp], lib_own
    )

    pl.semaphore_wait(barrier, tps - 1 + reps - 1)

    x_copy = copy(x_hbm, x_sib, x_send, x_recv, t=sib)
    x_copy.start()
    w_copies = {}
    for d, q in order:
        w_copies[d, q] = copy(
            w_columns(d, q, 1 - core), w_sib.at[d, q], w_send.at[d, q], w_recv.at[d, q], t=sib
        )

    def w_step(i):
        for key in order[4 * i:4 * i + 4]:
            w_copies[key].start()

    ready = set()

    def inputs(d, q):
        if not ready:
            x_load.wait()
            x_copy.wait_recv()
        if (d, q) not in ready:
            own_copies[d, q].wait()
            w_copies[d, q].wait_recv()
            ready.add((d, q))

    def partial(d, q, h=None):
        inputs(d, q)
        cols = slice(None) if h is None else pl.ds(h * half, half)
        return jnp.dot(x_ref[...], w_own[d, q, :, cols], preferred_element_type=F32) + jnp.dot(
            x_sib[...], w_sib[d, q, :, cols], preferred_element_type=F32
        )

    fars, dirs, accs, zs = {}, {}, {}, {}
    filled = set()

    def both_halves(buf, d, q):
        if (d, q) in filled:
            return
        filled.add((d, q))
        whole = partial(d, q).astype(BF)
        for h in range(2):
            buf[q, h] = whole[:, h * half:(h + 1) * half]

    def far_step(q, h):
        both_halves(s_far, 2, q)
        fars[q, h] = copy(
            s_far.at[q, h], r_far.at[q, h], far_send.at[q, h], far_recv.at[q, h],
            t=tp_of((x + way(q)) % NX, zl, core),
        )
        fars[q, h].start()

    def dir_step(q, h):
        d = NX - way(q)
        both_halves(s_dir, d, q)
        dirs[q, h] = copy(
            s_dir.at[q, h], r_dir.at[q, h], dir_send.at[q, h], dir_recv.at[q, h],
            t=tp_of((x + d) % NX, zl, core),
        )
        dirs[q, h].start()

    def acc_step(q, h):
        d = way(q)
        own = partial(d, q, h)
        fars[q, h].wait_recv()
        s_acc[q, h] = (own + r_far[q, h].astype(F32)).astype(BF)
        accs[q, h] = copy(
            s_acc.at[q, h], r_acc.at[q, h], acc_send.at[q, h], acc_recv.at[q, h],
            t=tp_of((x + d) % NX, zl, core),
        )
        accs[q, h].start()

    def z_step(q, h):
        own = partial(0, q, h)
        dirs[q, h].wait_recv()
        accs[q, h].wait_recv()
        total = own + r_dir[q, h].astype(F32) + r_acc[q, h].astype(F32)

        @pl.when(q == zl)
        def _():
            base[h] = total

        zs[q, h] = copy(
            s_z.at[q, h], r_z.at[zl, h], z_send.at[q, h], z_recv.at[zl, h], t=tp_of(x, q, core)
        )

        @pl.when(q != zl)
        def _():
            s_z[q, h] = total.astype(BF)
            zs[q, h].start()

    lib_all = copy(
        lib.at[pl.ds(0, tps - 1)], lib.at[pl.ds(0, tps - 1)], lib_send, lib_recv, t=sib
    )
    waits = []

    def lib_step():
        lib_copy.start()
        waits.append(lib_all)

        @pl.loop(1, tps)
        def _(j):
            to = (tp + j) % tps
            copy(
                a_ref.at[pl.ds(pl.multiple_of(to * width + y * share, share), share), :],
                lib.at[tp], lib_send, lib_recv, t=to,
            ).start()

    def choose_step():
        lib_copy.wait()
        lib_all.wait_recv()
        for j in range(1, NY):
            to = hi * NY + (y + j) % NY
            for p in range(prompts):
                s_sel[j, p] = lib[adapter_s[to * prompts + p]]
            c = copy(s_sel.at[j], sel.at[:, y], sel_send.at[j], sel_recv.at[y], r=to)
            c.start()
            waits.append(c)
        for p in range(prompts):
            sel[p, y] = lib[adapter_s[rep * prompts + p]]

    def chosen(p):
        return sel[p].reshape(width, sel.shape[3])

    rank = sel.shape[3] // 2
    thin = rows // NX
    line, place = NX * NC, x * NC + core

    def peer(j):
        other = (place + j) % line
        return other, tp_of(other // NC, zl, other % NC)

    def thin_rows(xx):
        return pl.ds(pl.multiple_of(xx * thin, thin), thin)

    def down_step():
        for j in range(1, NY):
            fr = (y + j) % NY
            copy(
                s_sel.at[j], sel.at[:, fr], sel_send.at[j], sel_recv.at[fr], r=hi * NY + fr
            ).wait_recv()
        for k in range(2):
            parts = [
                jnp.dot(
                    x_ref[pl.ds((2 * k + i) * rows, rows), :], chosen(2 * k + i),
                    preferred_element_type=F32,
                )
                for i in range(2)
            ]
            dpack[k] = jnp.concatenate([parts[0][:, :rank], parts[1][:, :rank]], axis=1)
        for j in range(1, line):
            other, to = peer(j)
            c = copy(
                dpack.at[other % NC, thin_rows(other // NC)], x_sum.at[place],
                down_send.at[j], down_recv.at[place], t=to,
            )
            c.start()
            waits.append(c)

    def down_z_step():
        total = dpack[core, thin_rows(x)]
        for j in range(1, line):
            other, to = peer(j)
            copy(
                dpack.at[core, thin_rows(x)], x_sum.at[other], down_send.at[j], down_recv.at[other], t=to
            ).wait_recv()
            total += x_sum[other]
        z_sum[zl] = total
        for j in range(1, NZ):
            c = copy(
                z_sum.at[zl], z_sum.at[zl], down_send.at[line + j], down_recv.at[line + zl],
                t=tp_of(x, (zl + j) % NZ, core),
            )
            c.start()
            waits.append(c)

    def down_back_step():
        for j in range(1, NZ):
            fr = (zl + j) % NZ
            copy(
                z_sum.at[fr], z_sum.at[fr], down_send.at[line + j], down_recv.at[line + fr],
                t=tp_of(x, fr, core),
            ).wait_recv()
        down[core, thin_rows(x)] = (z_sum[0] + z_sum[1]) + (z_sum[2] + z_sum[3])
        for j in range(1, line):
            other, to = peer(j)
            mine = down.at[core, thin_rows(x)]
            c = copy(
                mine, mine, down_send.at[line + NZ + j], down_recv.at[line + NZ + place], t=to
            )
            c.start()
            waits.append(c)

    def lift_step():
        for j in range(1, line):
            other, to = peer(j)
            theirs = down.at[other % NC, thin_rows(other // NC)]
            copy(
                theirs, theirs, down_send.at[line + NZ + j], down_recv.at[line + NZ + other], t=to
            ).wait_recv()
        lanes = lax.broadcasted_iota(jnp.int32, (rows, 2 * rank), 1)
        for p in range(prompts):
            pack = down[p // 2]
            if p % 2 == 0:
                pack = jnp.concatenate([pack[:, rank:], pack[:, :rank]], axis=1)
            pack = jnp.where(lanes >= rank, pack, 0.0).astype(BF)
            lift = 0.5 * lax.dot_general(
                pack, chosen(p), (((1,), (1,)), ((), ())), preferred_element_type=F32
            )
            for h in range(2):
                lifted[h, pl.ds(p * rows, rows), :] = lift[:, h * half:(h + 1) * half]

    outs = []

    def out_step(h):
        for j in range(1, NZ):
            fr = (zl + j) % NZ
            copy(
                s_z.at[0, h], r_z.at[fr, h], z_send.at[0, h], z_recv.at[fr, h], t=tp_of(x, fr, core)
            ).wait_recv()
        row_ids = lax.broadcasted_iota(jnp.int32, (rows, half), 0)
        results = []
        for p in range(prompts):
            span = pl.ds(p * rows, rows)
            total = base[h, span, :] + lifted[h, span, :]
            for j in range(1, NZ):
                total += r_z[(zl + j) % NZ, h, span, :].astype(F32)
            live = row_ids < lengths_s[rep * prompts + p]
            results.append(jnp.where(live, total, 0.0))
        cols = pl.ds(h * half, half)
        for j in FAR_FIRST:
            to = (hi + j // NY) % NH * NY + (y + j) % NY
            value = jnp.zeros((rows, half), F32)
            for p in range(prompts):
                value = jnp.where(target_s[rep * prompts + p] == to, results[p], value)
            if j == 0:
                out_ref[rep, :, cols] = value.astype(BF)
            else:
                s_out[j, h] = value.astype(BF)
                c = copy(
                    s_out.at[j, h], out_ref.at[rep, :, cols], out_send.at[j, h], out_recv.at[rep, h], r=to
                )
                c.start()
                outs.append(c)

    for c in tables:
        c.wait()
    rounds = [(h, pair) for h in range(2) for pair in pairs]
    base_steps = {"F": far_step, "D": dir_step, "C": acc_step, "S": z_step}
    other_steps = {
        "lib": lib_step, "choose": choose_step, "down": down_step,
        "down_z": down_z_step, "down_back": down_back_step, "lift": lift_step,
    }
    for step in SCHEDULE:
        if step[0] == "W":
            w_step(int(step[1]))
        elif step[0] in base_steps:
            h, pair = rounds[int(step[1])]
            for q in pair:
                base_steps[step[0]](q, h)
        elif step[0] == "O":
            out_step(int(step[1]))
        else:
            other_steps[step]()

    x_copy.wait_send()
    for c in w_copies.values():
        c.wait_send()
    for group in (fars, dirs, accs):
        for c in group.values():
            c.wait_send()
    for q in range(NZ):
        @pl.when(q != zl)
        def _(q=q):
            for h in range(2):
                zs[q, h].wait_send()
    for c in waits + outs:
        c.wait_send()
    for h in range(2):
        for j in range(1, reps):
            fr = (rep + j) % reps
            copy(
                s_out.at[j, h], out_ref.at[fr, :, pl.ds(h * half, half)],
                out_send.at[j, h], out_recv.at[fr, h], r=fr,
            ).wait_recv()


def local(prompts, output_matrix, adapter_weight_pair, adapter, lengths, placement):
    count, rows, width = prompts.shape
    reps = lax.axis_size("rep")
    tps = lax.axis_size("tp")
    pair = adapter_weight_pair.shape[2]
    tall = count * rows
    dma = pltpu.SemaphoreType.DMA
    vmem = pl.BlockSpec(memory_space=pltpu.VMEM)
    hbm = pl.BlockSpec(memory_space=pltpu.HBM)
    table = pltpu.SMEM((adapter.shape[0],), jnp.int32)
    block = pltpu.VMEM((NZ, 2, tall, width // 2), BF)
    out = pl.pallas_call(
        kernel,
        out_shape=jax.ShapeDtypeStruct((reps, rows, width), BF),
        in_specs=[hbm] * 6,
        out_specs=vmem,
        scratch_shapes=[
            table, table, table,
            pltpu.VMEM((tall, width), BF),
            pltpu.VMEM((tall, width), BF),
            pltpu.VMEM((NX, NZ, width, width), BF),
            pltpu.VMEM((NX, NZ, width, width), BF),
            block, block, block, block, block, block,
            block, block, pltpu.VMEM((2, tall, width // 2), F32),
            pltpu.VMEM((tps, width // NY, pair), BF),
            pltpu.VMEM((NY, count, width // NY, pair), BF),
            pltpu.VMEM((count, NY, width // NY, pair), BF),
            pltpu.VMEM((2, rows, pair), F32),
            pltpu.VMEM((NX * NC, rows // NX, pair), F32),
            pltpu.VMEM((NZ, rows // NX, pair), F32),
            pltpu.VMEM((2, rows, pair), F32),
            pltpu.VMEM((2, tall, width // 2), F32),
            pltpu.VMEM((reps, 2, rows, width // 2), BF),
            dma((4,)), dma((NX, NZ)), dma((NX, NZ)), dma((NX, NZ)), dma, dma,
            dma((NZ, 2)), dma((NZ, 2)), dma((NZ, 2)), dma((NZ, 2)), dma((NZ, 2)), dma((NZ, 2)),
            dma((NZ, 2)), dma((NZ, 2)),
            dma, dma, dma, dma((NY,)), dma((NY,)),
            dma((2 * NX * NC + NZ,)), dma((2 * NX * NC + NZ,)), dma((reps, 2)), dma((reps, 2)),
        ],
        compiler_params=pltpu.CompilerParams(
            collective_id=0, has_side_effects=True, vmem_limit_bytes=60 * 1024 * 1024
        ),
    )(
        adapter, lengths, placement.reshape(-1), prompts.reshape(tall, width), output_matrix,
        adapter_weight_pair.reshape(-1, pair),
    )
    return out[None]


def solution(mesh):
    in_specs = (P("rep", None, "tp"), P("tp", None), P("tp", None, None), P(), P(), P())
    out_specs = P("rep", None, None, "tp")
    return jax.shard_map(local, mesh=mesh, in_specs=in_specs, out_specs=out_specs, check_vma=False)
```

```python
import functools

import jax
import jax.numpy as jnp
from jax import lax
from jax.experimental import pallas as pl
from jax.experimental.pallas import tpu as pltpu
from jax.sharding import PartitionSpec as P

MESH = pl.DeviceIdType.MESH
BF = jnp.bfloat16
F32 = jnp.float32

NX, NZ, NC = 4, 4, 2
NY, NH = 4, 2
FAR_FIRST = (6, 5, 7, 4, 2, 1, 3, 0)
SCHEDULE = (
    "W0", "lib", "F0", "W1", "W2", "W3", "D0", "C0", "F1", "D1", "S0", "C1", "choose", "F2",
    "D2", "C2", "S1", "down", "F3", "D3", "S2", "down_z", "C3", "S3", "down_back", "lift", "O0", "O1",
)


def kernel(
    adapter_h, lengths_h, target_h, x_hbm, w_ref, a_ref, out_ref,
    adapter_s, lengths_s, target_s, x_ref, x_sib, w_own, w_sib,
    s_far, s_dir, s_acc, r_far, r_dir, r_acc,
    s_z, r_z, base,
    lib, s_sel, sel, dpack, x_sum, z_sum, down, lifted,
    s_out,
    in_sem, w_own_sem, w_send, w_recv, x_send, x_recv,
    far_send, far_recv, dir_send, dir_recv, acc_send, acc_recv,
    z_send, z_recv,
    lib_own, lib_send, lib_recv, sel_send, sel_recv,
    down_send, down_recv, out_send, out_recv,
):
    rep = lax.axis_index("rep")
    tp = lax.axis_index("tp")
    hi, y = rep // NY, rep % NY
    x = tp // (NZ * NC)
    zl = (tp // NC) % NZ
    core = tp % NC
    tps, reps = NX * NZ * NC, NY * NH
    prompts, rows = out_ref.shape[0] // 2, out_ref.shape[1]
    width = out_ref.shape[2]
    share, half = width // NY, width // 2

    def tp_of(xx, zz, cc):
        return (xx * NZ + zz) * NC + cc

    def copy(src, dst, send, recv, r=None, t=None):
        return pltpu.make_async_remote_copy(
            src_ref=src, dst_ref=dst, send_sem=send, recv_sem=recv,
            device_id=(rep if r is None else r, tp if t is None else t),
            device_id_type=MESH,
        )

    sib = tp_of(x, zl, 1 - core)

    barrier = pltpu.get_barrier_semaphore()

    @pl.loop(1, tps)
    def _(j):
        pl.semaphore_signal(barrier, inc=1, device_id=(rep, (tp + j) % tps), device_id_type=MESH)

    @pl.loop(1, reps)
    def _(j):
        pl.semaphore_signal(barrier, inc=1, device_id=((rep + j) % reps, tp), device_id_type=MESH)

    def w_columns(d, q, cc):
        start = tp_of((x + d) % NX, q, cc) * width
        return w_ref.at[:, pl.ds(pl.multiple_of(start, width), width)]

    def way(q):
        return 1 if q < NZ // 2 else 3

    pairs = ((0, 3), (1, 2))
    order = []
    for pair in pairs:
        order += [(2, q) for q in pair] + [(NX - way(q), q) for q in pair]
    for pair in pairs:
        order += [(way(q), q) for q in pair]
    order += [(0, q) for pair in pairs for q in pair]
    x_load = pltpu.make_async_copy(x_hbm, x_ref, in_sem.at[0])
    x_load.start()
    tables = [
        pltpu.make_async_copy(src, dst, in_sem.at[i + 1])
        for i, (src, dst) in enumerate(
            ((adapter_h, adapter_s), (lengths_h, lengths_s), (target_h, target_s))
        )
    ]
    for c in tables:
        c.start()
    own_copies = {}
    for d, q in order:
        own_copies[d, q] = pltpu.make_async_copy(
            w_columns(d, q, core), w_own.at[d, q], w_own_sem.at[d, q]
        )
        own_copies[d, q].start()
    lib_copy = pltpu.make_async_copy(
        a_ref.at[pl.ds(pl.multiple_of(tp * width + y * share, share), share), :], lib.at[tp], lib_own
    )

    pl.semaphore_wait(barrier, tps - 1 + reps - 1)

    x_copy = copy(x_hbm, x_sib, x_send, x_recv, t=sib)
    x_copy.start()
    w_copies = {}
    for d, q in order:
        w_copies[d, q] = copy(
            w_columns(d, q, 1 - core), w_sib.at[d, q], w_send.at[d, q], w_recv.at[d, q], t=sib
        )

    def w_step(i):
        for key in order[4 * i:4 * i + 4]:
            w_copies[key].start()

    ready = set()

    def inputs(d, q):
        if not ready:
            x_load.wait()
            x_copy.wait_recv()
        if (d, q) not in ready:
            own_copies[d, q].wait()
            w_copies[d, q].wait_recv()
            ready.add((d, q))

    def partial(d, q, h=None):
        inputs(d, q)
        cols = slice(None) if h is None else pl.ds(h * half, half)
        return jnp.dot(x_ref[...], w_own[d, q, :, cols], preferred_element_type=F32) + jnp.dot(
            x_sib[...], w_sib[d, q, :, cols], preferred_element_type=F32
        )

    fars, dirs, accs, zs = {}, {}, {}, {}
    filled = set()

    def both_halves(buf, d, q):
        if (d, q) in filled:
            return
        filled.add((d, q))
        whole = partial(d, q).astype(BF)
        for h in range(2):
            buf[q, h] = whole[:, h * half:(h + 1) * half]

    def far_step(q, h):
        both_halves(s_far, 2, q)
        fars[q, h] = copy(
            s_far.at[q, h], r_far.at[q, h], far_send.at[q, h], far_recv.at[q, h],
            t=tp_of((x + way(q)) % NX, zl, core),
        )
        fars[q, h].start()

    def dir_step(q, h):
        d = NX - way(q)
        both_halves(s_dir, d, q)
        dirs[q, h] = copy(
            s_dir.at[q, h], r_dir.at[q, h], dir_send.at[q, h], dir_recv.at[q, h],
            t=tp_of((x + d) % NX, zl, core),
        )
        dirs[q, h].start()

    def acc_step(q, h):
        d = way(q)
        own = partial(d, q, h)
        fars[q, h].wait_recv()
        s_acc[q, h] = (own + r_far[q, h].astype(F32)).astype(BF)
        accs[q, h] = copy(
            s_acc.at[q, h], r_acc.at[q, h], acc_send.at[q, h], acc_recv.at[q, h],
            t=tp_of((x + d) % NX, zl, core),
        )
        accs[q, h].start()

    def z_step(q, h):
        own = partial(0, q, h)
        dirs[q, h].wait_recv()
        accs[q, h].wait_recv()
        total = own + r_dir[q, h].astype(F32) + r_acc[q, h].astype(F32)

        @pl.when(q == zl)
        def _():
            base[h] = total

        zs[q, h] = copy(
            s_z.at[q, h], r_z.at[zl, h], z_send.at[q, h], z_recv.at[zl, h], t=tp_of(x, q, core)
        )

        @pl.when(q != zl)
        def _():
            s_z[q, h] = total.astype(BF)
            zs[q, h].start()

    lib_all = copy(
        lib.at[pl.ds(0, tps - 1)], lib.at[pl.ds(0, tps - 1)], lib_send, lib_recv, t=sib
    )
    waits = []

    def lib_step():
        lib_copy.start()
        waits.append(lib_all)

        @pl.loop(1, tps)
        def _(j):
            to = (tp + j) % tps
            copy(
                a_ref.at[pl.ds(pl.multiple_of(to * width + y * share, share), share), :],
                lib.at[tp], lib_send, lib_recv, t=to,
            ).start()

    def choose_step():
        lib_copy.wait()
        lib_all.wait_recv()
        for j in range(1, NY):
            to = hi * NY + (y + j) % NY
            for p in range(prompts):
                s_sel[j, p] = lib[adapter_s[to * prompts + p]]
            c = copy(s_sel.at[j], sel.at[:, y], sel_send.at[j], sel_recv.at[y], r=to)
            c.start()
            waits.append(c)
        for p in range(prompts):
            sel[p, y] = lib[adapter_s[rep * prompts + p]]

    def chosen(p):
        return sel[p].reshape(width, sel.shape[3])

    rank = sel.shape[3] // 2
    thin = rows // NX
    line, place = NX * NC, x * NC + core

    def peer(j):
        other = (place + j) % line
        return other, tp_of(other // NC, zl, other % NC)

    def thin_rows(xx):
        return pl.ds(pl.multiple_of(xx * thin, thin), thin)

    def down_step():
        for j in range(1, NY):
            fr = (y + j) % NY
            copy(
                s_sel.at[j], sel.at[:, fr], sel_send.at[j], sel_recv.at[fr], r=hi * NY + fr
            ).wait_recv()
        for k in range(2):
            parts = [
                jnp.dot(
                    x_ref[pl.ds((2 * k + i) * rows, rows), :], chosen(2 * k + i),
                    preferred_element_type=F32,
                )
                for i in range(2)
            ]
            dpack[k] = jnp.concatenate([parts[0][:, :rank], parts[1][:, :rank]], axis=1)
        for j in range(1, line):
            other, to = peer(j)
            c = copy(
                dpack.at[other % NC, thin_rows(other // NC)], x_sum.at[place],
                down_send.at[j], down_recv.at[place], t=to,
            )
            c.start()
            waits.append(c)

    def down_z_step():
        total = dpack[core, thin_rows(x)]
        for j in range(1, line):
            other, to = peer(j)
            copy(
                dpack.at[core, thin_rows(x)], x_sum.at[other], down_send.at[j], down_recv.at[other], t=to
            ).wait_recv()
            total += x_sum[other]
        z_sum[zl] = total
        for j in range(1, NZ):
            c = copy(
                z_sum.at[zl], z_sum.at[zl], down_send.at[line + j], down_recv.at[line + zl],
                t=tp_of(x, (zl + j) % NZ, core),
            )
            c.start()
            waits.append(c)

    def down_back_step():
        for j in range(1, NZ):
            fr = (zl + j) % NZ
            copy(
                z_sum.at[fr], z_sum.at[fr], down_send.at[line + j], down_recv.at[line + fr],
                t=tp_of(x, fr, core),
            ).wait_recv()
        down[core, thin_rows(x)] = (z_sum[0] + z_sum[1]) + (z_sum[2] + z_sum[3])
        for j in range(1, line):
            other, to = peer(j)
            mine = down.at[core, thin_rows(x)]
            c = copy(
                mine, mine, down_send.at[line + NZ + j], down_recv.at[line + NZ + place], t=to
            )
            c.start()
            waits.append(c)

    def lift_step():
        for j in range(1, line):
            other, to = peer(j)
            theirs = down.at[other % NC, thin_rows(other // NC)]
            copy(
                theirs, theirs, down_send.at[line + NZ + j], down_recv.at[line + NZ + other], t=to
            ).wait_recv()
        lanes = lax.broadcasted_iota(jnp.int32, (rows, 2 * rank), 1)
        for p in range(prompts):
            pack = down[p // 2]
            if p % 2 == 0:
                pack = jnp.concatenate([pack[:, rank:], pack[:, :rank]], axis=1)
            pack = jnp.where(lanes >= rank, pack, 0.0).astype(BF)
            lift = 0.5 * lax.dot_general(
                pack, chosen(p), (((1,), (1,)), ((), ())), preferred_element_type=F32
            )
            for h in range(2):
                lifted[h, pl.ds(p * rows, rows), :] = lift[:, h * half:(h + 1) * half]

    outs, kept = [], []

    def out_step(h):
        for j in range(1, NZ):
            fr = (zl + j) % NZ
            copy(
                s_z.at[0, h], r_z.at[fr, h], z_send.at[0, h], z_recv.at[fr, h], t=tp_of(x, fr, core)
            ).wait_recv()
        row_ids = lax.broadcasted_iota(jnp.int32, (rows, half), 0)
        results = []
        for p in range(prompts):
            span = pl.ds(p * rows, rows)
            total = base[h, span, :] + lifted[h, span, :]
            for j in range(1, NZ):
                total += r_z[(zl + j) % NZ, h, span, :].astype(F32)
            live = row_ids < lengths_s[rep * prompts + p]
            results.append(jnp.where(live, total, 0.0))
        cols = pl.ds(h * half, half)
        for j in FAR_FIRST:
            to = (hi + j // NY) % NH * NY + (y + j) % NY
            value = jnp.zeros((rows, half), F32)
            for p in range(prompts):
                value = jnp.where(target_s[rep * prompts + p] == to, results[p], value)
            if j == 0:
                s_out[0, h] = value.astype(BF)
                c = pltpu.make_async_copy(s_out.at[0, h], out_ref.at[rep, :, cols], out_send.at[0, h])
                c.start()
                kept.append(c)
            else:
                s_out[j, h] = value.astype(BF)
                c = copy(
                    s_out.at[j, h], out_ref.at[rep, :, cols], out_send.at[j, h], out_recv.at[rep, h], r=to
                )
                c.start()
                outs.append(c)

    for c in tables:
        c.wait()
    rounds = [(h, pair) for h in range(2) for pair in pairs]
    base_steps = {"F": far_step, "D": dir_step, "C": acc_step, "S": z_step}
    other_steps = {
        "lib": lib_step, "choose": choose_step, "down": down_step,
        "down_z": down_z_step, "down_back": down_back_step, "lift": lift_step,
    }
    for step in SCHEDULE:
        if step[0] == "W":
            w_step(int(step[1]))
        elif step[0] in base_steps:
            h, pair = rounds[int(step[1])]
            for q in pair:
                base_steps[step[0]](q, h)
        elif step[0] == "O":
            out_step(int(step[1]))
        else:
            other_steps[step]()

    x_copy.wait_send()
    for c in w_copies.values():
        c.wait_send()
    for group in (fars, dirs, accs):
        for c in group.values():
            c.wait_send()
    for q in range(NZ):
        @pl.when(q != zl)
        def _(q=q):
            for h in range(2):
                zs[q, h].wait_send()
    for c in waits + outs:
        c.wait_send()
    for c in kept:
        c.wait()
    for h in range(2):
        for j in range(1, reps):
            fr = (rep + j) % reps
            copy(
                s_out.at[j, h], out_ref.at[fr, :, pl.ds(h * half, half)],
                out_send.at[j, h], out_recv.at[fr, h], r=fr,
            ).wait_recv()


def local(prompts, output_matrix, adapter_weight_pair, adapter, lengths, placement):
    count, rows, width = prompts.shape
    reps = lax.axis_size("rep")
    tps = lax.axis_size("tp")
    pair = adapter_weight_pair.shape[2]
    tall = count * rows
    dma = pltpu.SemaphoreType.DMA
    hbm = pl.BlockSpec(memory_space=pltpu.HBM)
    table = pltpu.SMEM((adapter.shape[0],), jnp.int32)
    block = pltpu.VMEM((NZ, 2, tall, width // 2), BF)
    out = pl.pallas_call(
        kernel,
        out_shape=jax.ShapeDtypeStruct((reps, rows, width), BF),
        in_specs=[hbm] * 6,
        out_specs=hbm,
        scratch_shapes=[
            table, table, table,
            pltpu.VMEM((tall, width), BF),
            pltpu.VMEM((tall, width), BF),
            pltpu.VMEM((NX, NZ, width, width), BF),
            pltpu.VMEM((NX, NZ, width, width), BF),
            block, block, block, block, block, block,
            block, block, pltpu.VMEM((2, tall, width // 2), F32),
            pltpu.VMEM((tps, width // NY, pair), BF),
            pltpu.VMEM((NY, count, width // NY, pair), BF),
            pltpu.VMEM((count, NY, width // NY, pair), BF),
            pltpu.VMEM((2, rows, pair), F32),
            pltpu.VMEM((NX * NC, rows // NX, pair), F32),
            pltpu.VMEM((NZ, rows // NX, pair), F32),
            pltpu.VMEM((2, rows, pair), F32),
            pltpu.VMEM((2, tall, width // 2), F32),
            pltpu.VMEM((reps, 2, rows, width // 2), BF),
            dma((4,)), dma((NX, NZ)), dma((NX, NZ)), dma((NX, NZ)), dma, dma,
            dma((NZ, 2)), dma((NZ, 2)), dma((NZ, 2)), dma((NZ, 2)), dma((NZ, 2)), dma((NZ, 2)),
            dma((NZ, 2)), dma((NZ, 2)),
            dma, dma, dma, dma((NY,)), dma((NY,)),
            dma((2 * NX * NC + NZ,)), dma((2 * NX * NC + NZ,)), dma((reps, 2)), dma((reps, 2)),
        ],
        compiler_params=pltpu.CompilerParams(
            collective_id=0, has_side_effects=True, vmem_limit_bytes=60 * 1024 * 1024
        ),
    )(
        adapter, lengths, placement.reshape(-1), prompts.reshape(tall, width), output_matrix,
        adapter_weight_pair.reshape(-1, pair),
    )
    return out[None]


def solution(mesh):
    in_specs = (P("rep", None, "tp"), P("tp", None), P("tp", None, None), P(), P(), P())
    out_specs = P("rep", None, None, "tp")
    return jax.shard_map(local, mesh=mesh, in_specs=in_specs, out_specs=out_specs, check_vma=False)
```
